256 devices in a mesh: tok: 32 (over x, z_hi, core), col: 8 (over z_lo, y).
Axes of the slice: x: 4, y: 4, z: 8 (z_hi: 4, z_lo: 2; z = z_hi * 2 + z_lo), core: 2. Of those that a mesh axis runs over, the one named last changes fastest.
Arguments:
- residual_rows: bfloat16 [1024, 16384], P('col', 'tok'), may hold values from -6 to 6
- basis: bfloat16 [16384, 16384], P('tok', 'col'), may hold values from -0.046875 to 0.046875
Outputs:
- covariance: float32 [16384, 16384], P('col', 'tok')
The draws below stay inside these ranges and needn't reach their ends.
All inputs are finite; a program needn't handle non-finite values.
Results may differ from the reference program's by a relative error of at most 0.0038.
Values may be sent and summed in bfloat16 or wider, within the bound.
A program may use at most 64 MiB of HBM per device.

```python
import jax
import jax.numpy as jnp
from jax import lax

D = 16384
TOKENS = 1024


def block_levels(rng, extent, shards, low, top_value):
    level, own = 1.0, jax.random.fold_in(rng, 6)
    for position, blocks in shards:
        draws = jnp.exp(jax.random.uniform(jax.random.fold_in(own, position), (blocks,), jnp.float32, low / len(shards), top_value / len(shards)))
        level = level * jnp.repeat(draws, extent[position] // blocks).reshape([-1 if axis == position else 1 for axis in range(len(extent))])
    return level


def centred(own_key, dims, deviation, most, split=(), kind=jnp.bfloat16):
    array = jax.random.normal(own_key, dims, jnp.float32) * deviation
    if len(split) > 0:
        array = block_levels(own_key, dims, split, -0.22, 0.18) * array
    return jnp.clip(array, min=-most, max=most).astype(kind)


def setup_inputs(seed: int = 0) -> dict:
    seeds = jax.random.split(jax.random.key(seed), 3)
    return {
        "residual_rows": centred(seeds[0], (TOKENS, D), 1.0, 6.0, ((0, 8), (1, 32))),
        "basis": centred(seeds[1], (D, D), D ** -0.5, 0.046875, ((0, 32), (1, 8))),
    }


def reference(residual_rows, basis):
    width = basis.shape[0]
    blocks = width // 2048 if width % 2048 == 0 and width >= 2048 else 1
    step_cols = width // blocks
    rows_float = residual_rows.astype(jnp.float32)

    def rotate_block(index):
        cols = lax.dynamic_slice_in_dim(basis, (index * step_cols).astype(jnp.int32), step_cols, 1)
        return jnp.dot(rows_float, cols.astype(jnp.float32)).astype(jnp.bfloat16)

    pieces = lax.map(rotate_block, jnp.arange(blocks, dtype=jnp.int32))
    rotated = jnp.transpose(pieces, (1, 0, 2)).reshape(residual_rows.shape[0], width)
    rotated_float = rotated.astype(jnp.float32)

    def cov_block(index):
        cols = lax.dynamic_slice_in_dim(rotated_float, (index * step_cols).astype(jnp.int32), step_cols, 1)
        return jnp.dot(rotated_float.T, cols) / residual_rows.shape[0]

    tiles = lax.map(cov_block, jnp.arange(blocks, dtype=jnp.int32))
    return jnp.transpose(tiles, (1, 0, 2)).reshape(width, width)
```

```python
import jax
import jax.numpy as jnp
from jax import lax
from jax.experimental import pallas as pl
from jax.experimental.pallas import tpu as pltpu
from jax.sharding import PartitionSpec as P

MESH = pl.DeviceIdType.MESH
F32, BF16 = jnp.float32, jnp.bfloat16

BLOCKS = 4
X_FIRST = (True, True, False, True)
UP, DOWN = 2.0**50, 2.0**-50


def pack(value):
    scaled = value * UP
    return (scaled * jnp.abs(scaled)).astype(BF16)


def unpack(code):
    code = code.astype(F32)
    return code * lax.rsqrt(jnp.maximum(jnp.abs(code), 2.0**-126)) * DOWN


def device(x, z, k, w, y):
    return ((x * 4 + z) * 2 + k, w * 4 + y)


def other(i):
    return i + 1 - 2 * (i % 2)


def kernel(
    r_ref, b_ref, yt, yp,
    rx, bf, part, acc, s1, r1, s2, r2, s3, r3, s4, r4,
    in_sem, rs_send, rs_recv, ag_send, ag_recv, fw_send, fw_recv, pn_send, pn_recv,
):
    t, c = lax.axis_index("tok"), lax.axis_index("col")
    x, z, k, w, y = t // 8, (t // 2) % 4, t % 2, c // 4, c % 4
    core = device(x, z, 1 - k, w, y)
    pair = device(x, z, k, 1 - w, y)
    diag = device(x, z, 1 - k, 1 - w, y)
    y_peers = [device(x, z, k, w, (y + d) % 4) for d in (1, 3, 2)]
    x_peers = [device(other(x), z, k, w, y), device(3 - x, z, k, w, y)]
    z_peers = [device(x, other(z), k, w, y), device(x, 3 - z, k, w, y)]
    panel_to = device(2 * w + y // 2, 2 * (y % 2) + x // 2, x % 2, k, (z + 2) % 4)
    src_w, src_y, src_z = x // 2, (x % 2) * 2 + z // 2, (y + 2) % 4
    panel_from = device((z % 2) * 2 + k, src_z, w, src_w, src_y)
    sends = []

    def remote(src, dst, send, recv, to):
        return pltpu.make_async_remote_copy(
            src_ref=src, dst_ref=dst, send_sem=send, recv_sem=recv, device_id=to, device_id_type=MESH
        )

    def start(*args):
        copy = remote(*args)
        copy.start()
        sends.append(copy)

    def wait(dst, recv):
        remote(dst, dst, recv, recv, core).wait_recv()

    own_rows = pl.ds(pl.multiple_of(k * 512, 512), 512)
    peer_rows = pl.ds(pl.multiple_of((1 - k) * 512, 512), 512)
    own_b = pltpu.make_async_copy(b_ref, bf.at[own_rows], in_sem.at[0])
    own_b.start()

    barrier = pltpu.get_barrier_semaphore()
    partners = [core, pair, diag, *y_peers, *x_peers, *z_peers, panel_to, panel_from]
    for d in partners:
        pl.semaphore_signal(barrier, inc=1, device_id=d, device_id_type=MESH)
    pl.semaphore_wait(barrier, len(partners))

    r_own = rx.at[0, :, own_rows]
    r_peer = rx.at[0, :, peer_rows]
    keep = pltpu.make_async_copy(r_ref, r_own, in_sem.at[1])
    across = remote(r_ref, r_own, in_sem.at[2], in_sem.at[3 + k], device(x, z, w, 1 - w, y))
    beside = remote(r_ref, r_own, in_sem.at[5], in_sem.at[3 + k], core)
    across.start()

    @pl.when(k == w)
    def _():
        keep.start()

    @pl.when(k != w)
    def _():
        beside.start()

    order = [(x + 2) % 4, other(x), 3 - x, x]
    for i, o in enumerate(order):
        cols = pl.ds(pl.multiple_of(o * 512, 512), 512)
        start(b_ref.at[:, cols], bf.at[own_rows, cols], in_sem.at[6 + i], in_sem.at[10 + i], core)

    wait(r_peer, in_sem.at[3 + 1 - k])

    @pl.when(k == w)
    def _():
        keep.wait()

    @pl.when(k != w)
    def _():
        wait(r_own, in_sem.at[3 + k])
        beside.wait_send()

    for i, d in enumerate(y_peers):
        start(rx.at[0], rx.at[1 + i], in_sem.at[14 + i], in_sem.at[17 + i], d)
    own_b.wait()

    axes = {True: (x, x_peers), False: (z, z_peers)}

    def piece(block, first, second, half):
        rows = pl.ds(64 * half, 64)
        if X_FIRST[block]:
            return part.at[block, first, :, rows, :] if second is None else part.at[block, first, second, rows, :]
        return part.at[block, :, first, rows, :] if second is None else part.at[block, second, first, rows, :]

    def roles(i, half):
        pairs = (other(i), 3 - i) if half == 0 else (3 - i, other(i))
        return i, pairs[0], pairs[1], (i + 2) % 4

    def rs_sems(block, half, i):
        n = (block * 2 + half) * 6 + i
        return rs_send.at[n], rs_recv.at[n]

    def dots(block):
        if block > 0:
            wait(rx.at[block], in_sem.at[17 + block - 1])
        i1, peers = axes[X_FIRST[block]]
        for n, o in enumerate(order):
            cols = pl.ds(pl.multiple_of(o * 512, 512), 512)
            if block == 0:
                wait(bf.at[peer_rows, cols], in_sem.at[10 + n])
            out = jnp.dot(rx[block], bf[:, cols], preferred_element_type=F32)
            for q in range(4):
                part[block, o, q] = out[:, q * 128 : (q + 1) * 128]
            if X_FIRST[block] and n < 3:
                first_sends(block, n)
        if not X_FIRST[block]:
            for n in range(3):
                first_sends(block, n)

    def first_sends(block, n):
        i1, peers = axes[X_FIRST[block]]
        for half in range(2):
            me, p1, p2, opp = roles(i1, half)
            slot = 0 if n == 0 else (1 if n == 1 + half else None)
            if slot is None:
                continue
            s1[block, half, slot] = pack(piece(block, (opp, p1)[slot], None, half)[...])
            start(s1.at[block, half, slot], r1.at[block, half, slot], *rs_sems(block, half, slot), peers[half])

    def second(block):
        i1, peers = axes[X_FIRST[block]]
        for half in range(2):
            me, p1, p2, opp = roles(i1, half)
            wait(r1.at[block, half, 0], rs_sems(block, half, 0)[1])
            s2[block, half] = pack(piece(block, p2, None, half)[...] + unpack(r1[block, half, 0]))
            start(s2.at[block, half], r2.at[block, half], *rs_sems(block, half, 2), peers[1 - half])

    def third(block):
        i1, _ = axes[X_FIRST[block]]
        i2, peers = axes[not X_FIRST[block]]
        for half in range(2):
            me = i1
            wait(r1.at[block, half, 1], rs_sems(block, half, 1)[1])
            wait(r2.at[block, half], rs_sems(block, half, 2)[1])
            acc[block, half] = (
                piece(block, me, None, half)[...] + unpack(r1[block, half, 1]) + unpack(r2[block, half])
            )
            me, p1, p2, opp = roles(i2, half)
            for slot, o in enumerate((opp, p1)):
                s3[block, half, slot] = pack(acc[block, half, o])
                start(s3.at[block, half, slot], r3.at[block, half, slot], *rs_sems(block, half, 3 + slot), peers[half])

    def fourth(block):
        i2, peers = axes[not X_FIRST[block]]
        for half in range(2):
            me, p1, p2, opp = roles(i2, half)
            wait(r3.at[block, half, 0], rs_sems(block, half, 3)[1])
            s4[block, half] = pack(acc[block, half, p2] + unpack(r3[block, half, 0]))
            start(s4.at[block, half], r4.at[block, half], *rs_sems(block, half, 5), peers[1 - half])

    def token_lanes(half, place):
        return pl.ds(pl.multiple_of(half * 512 + place * 128, 128), 128)

    shifts = (0, 3, 1, 2)

    def mine(block):
        return token_lanes(k, (y + shifts[block]) % 4)

    def fifth(block):
        i2, _ = axes[not X_FIRST[block]]
        done = []
        for half in range(2):
            wait(r3.at[block, half, 1], rs_sems(block, half, 4)[1])
            wait(r4.at[block, half], rs_sems(block, half, 5)[1])
            done.append(acc[block, half, i2] + unpack(r3[block, half, 1]) + unpack(r4[block, half]))
        flat = jnp.concatenate(done, axis=0).T.astype(BF16)
        for half in range(2):
            yt[x, z, half, :, mine(block)] = flat[64 * half : 64 * half + 64]

    def ag_sems(block, half, i):
        n = (block * 2 + half) * 6 + i
        return ag_send.at[n], ag_recv.at[n]

    def spot(block, half, inner, outer):
        a, b = (outer, inner) if X_FIRST[block] else (inner, outer)
        a = slice(None) if a is None else a
        b = slice(None) if b is None else b
        return yt.at[a, b, half, :, mine(block)]

    def gather_send(block, half, i, inner, outer, to):
        ref = spot(block, half, inner, outer)
        start(ref, ref, *ag_sems(block, half, i), to)

    def gather_wait(block, half, i, inner, outer):
        wait(spot(block, half, inner, outer), ag_sems(block, half, i)[1])

    def forward(block, i, ref):
        start(ref, ref, fw_send.at[block * 7 + i], fw_recv.at[block * 7 + i], core)

    def gather1(block):
        (ii, peers), (oi, _) = axes[not X_FIRST[block]], axes[X_FIRST[block]]
        for half in range(2):
            gather_send(block, half, 0, ii, oi, peers[half])

    def gather2(block):
        (ii, peers), (oi, _) = axes[not X_FIRST[block]], axes[X_FIRST[block]]
        for half in range(2):
            me, p1, p2, opp = roles(ii, half)
            gather_send(block, half, 1, me, oi, peers[1 - half])
            gather_wait(block, half, 0, p1, oi)
            gather_send(block, half, 2, p1, oi, peers[1 - half])

    def gather3(block):
        (ii, _), (oi, peers) = axes[not X_FIRST[block]], axes[X_FIRST[block]]
        for half in range(2):
            me, p1, p2, opp = roles(ii, half)
            gather_wait(block, half, 1, p2, oi)
            gather_wait(block, half, 2, opp, oi)
            gather_send(block, half, 3, None, oi, peers[half])
        a, b = (oi, slice(None)) if X_FIRST[block] else (slice(None), oi)
        forward(block, 0, yt.at[a, b, :, :, mine(block)])

    def gather4(block):
        oi, peers = axes[X_FIRST[block]]
        for half in range(2):
            me, p1, p2, opp = roles(oi, half)
            gather_send(block, half, 4, None, me, peers[1 - half])
            gather_wait(block, half, 3, None, p1)
            gather_send(block, half, 5, None, p1, peers[1 - half])
            forward(block, 1 + half, spot(block, half, None, p1))

    def gather5(block):
        oi, peers = axes[X_FIRST[block]]
        for half in range(2):
            me, p1, p2, opp = roles(oi, half)
            gather_wait(block, half, 4, None, p2)
            forward(block, 3 + half, spot(block, half, None, p2))
            gather_wait(block, half, 5, None, opp)
            forward(block, 5 + half, spot(block, half, None, opp))

    def forwarded(block):
        lanes = token_lanes(1 - k, (y + shifts[block]) % 4)
        (ii, _), (oi, _) = axes[not X_FIRST[block]], axes[X_FIRST[block]]
        a, b = (oi, slice(None)) if X_FIRST[block] else (slice(None), oi)
        wait(yt.at[a, b, :, :, lanes], fw_recv.at[block * 7])
        for half in range(2):
            me, p1, p2, opp = roles(oi, half)
            for i, o in ((1, p1), (3, p2), (5, opp)):
                a, b = (o, slice(None)) if X_FIRST[block] else (slice(None), o)
                wait(yt.at[a, b, half, :, lanes], fw_recv.at[block * 7 + i + half])

    def pn_sems(block, i):
        return pn_send.at[block * 8 + i], pn_recv.at[block * 8 + i]

    def panel_spot(block, source, half):
        return yp.at[source, :, :, token_lanes(half, (src_y + shifts[block]) % 4)]

    def panel1(block):
        start(yt.at[x, z, :, :, mine(block)], yp.at[z, :, :, mine(block)], *pn_sems(block, 0), panel_to)

    def panel2(block):
        ref = panel_spot(block, src_z, w)
        wait(ref, pn_sems(block, 0)[1])
        start(ref, ref, *pn_sems(block, 1), pair)
        for i, d in enumerate(y_peers):
            start(ref, ref, *pn_sems(block, 2 + i), d)

    def panel3(block):
        ref = panel_spot(block, src_z, 1 - w)
        wait(ref, pn_sems(block, 1)[1])
        for i, d in enumerate(y_peers):
            start(ref, ref, *pn_sems(block, 5 + i), d)

    def panel4(block):
        for i, shift in enumerate((3, 1, 2)):
            source = (y + shift + 2) % 4
            wait(panel_spot(block, source, w), pn_sems(block, 2 + i)[1])
            wait(panel_spot(block, source, 1 - w), pn_sems(block, 5 + i)[1])

    def finish(block):
        fifth(block)
        gather1(block)
        panel1(block)

    plan = [
        (dots, 0), (second, 0), (third, 0), (dots, 1), (dots, 2), (fourth, 0), (second, 1), (second, 2), (finish, 0),
        (dots, 3), (third, 1), (third, 2), (gather2, 0), (panel2, 0), (second, 3), (fourth, 1), (fourth, 2),
        (gather3, 0), (panel3, 0), (third, 3), (finish, 1), (finish, 2), (gather4, 0), (fourth, 3),
        (gather2, 1), (gather2, 2), (panel2, 1), (panel2, 2), (finish, 3), (gather3, 1), (gather3, 2),
        (panel3, 1), (panel3, 2), (gather2, 3), (panel2, 3), (gather4, 1), (gather4, 2), (gather3, 3), (panel3, 3),
        (gather5, 0), (gather4, 3), (gather5, 1), (gather5, 2), (gather5, 3),
    ]
    for step, block in plan:
        step(block)
    for block in range(BLOCKS):
        panel4(block)
        forwarded(block)
    across.wait_send()
    for copy in sends:
        copy.wait_send()


def rotate(residual_rows, basis):
    dma = pltpu.SemaphoreType.DMA
    return pl.pallas_call(
        kernel,
        out_shape=[jax.ShapeDtypeStruct((4, 4, 2, 64, 1024), BF16), jax.ShapeDtypeStruct((4, 2, 64, 1024), BF16)],
        in_specs=[pl.BlockSpec(memory_space=pltpu.VMEM), pl.BlockSpec(memory_space=pl.ANY)],
        out_specs=[pl.BlockSpec(memory_space=pltpu.VMEM)] * 2,
        scratch_shapes=[
            pltpu.VMEM((BLOCKS, 128, 1024), BF16),
            pltpu.VMEM((1024, 2048), BF16),
            pltpu.VMEM((BLOCKS, 4, 4, 128, 128), F32),
            pltpu.VMEM((BLOCKS, 2, 4, 64, 128), F32),
            pltpu.VMEM((BLOCKS, 2, 2, 4, 64, 128), BF16),
            pltpu.VMEM((BLOCKS, 2, 2, 4, 64, 128), BF16),
            pltpu.VMEM((BLOCKS, 2, 4, 64, 128), BF16),
            pltpu.VMEM((BLOCKS, 2, 4, 64, 128), BF16),
            pltpu.VMEM((BLOCKS, 2, 2, 64, 128), BF16),
            pltpu.VMEM((BLOCKS, 2, 2, 64, 128), BF16),
            pltpu.VMEM((BLOCKS, 2, 64, 128), BF16),
            pltpu.VMEM((BLOCKS, 2, 64, 128), BF16),
            dma((20,)),
            dma((BLOCKS * 12,)),
            dma((BLOCKS * 12,)),
            dma((BLOCKS * 12,)),
            dma((BLOCKS * 12,)),
            dma((BLOCKS * 7,)),
            dma((BLOCKS * 7,)),
            dma((BLOCKS * 8,)),
            dma((BLOCKS * 8,)),
        ],
        compiler_params=pltpu.CompilerParams(collective_id=0, has_side_effects=True, vmem_limit_bytes=48 * 2**20),
        cost_estimate=pl.CostEstimate(flops=2**31, bytes_accessed=8 * 2**20, transcendentals=0),
    )(residual_rows, basis)


def body(residual_rows, basis):
    columns, panel = rotate(residual_rows, basis)
    tile = lax.dot_general(
        columns.reshape(2048, 1024),
        panel.reshape(512, 1024),
        (((1,), (1,)), ((), ())),
        preferred_element_type=F32,
    )
    return tile * (1.0 / 1024)


def solution(mesh):
    return jax.shard_map(
        body,
        mesh=mesh,
        in_specs=(P("col", "tok"), P("tok", "col")),
        out_specs=P("col", "tok"),
        check_vma=False,
    )
```

```python
import jax
import jax.numpy as jnp
from jax import lax
from jax.experimental import pallas as pl
from jax.experimental.pallas import tpu as pltpu
from jax.sharding import PartitionSpec as P

MESH = pl.DeviceIdType.MESH
F32, BF16 = jnp.float32, jnp.bfloat16

SHIFTS = (0, 0, 2, 3, 1, 3, 1, 2)
CROSS = (0, 1, 0, 0, 0, 1, 1, 1)
X_FIRST = (True, True, True, False, True, True, True, True)
SUM_DIRECT = (False, False, False, False, False, False, False, False)
GATHER_DIRECT = (False, False, False, False, False, False, False, False)
BLOCKS = 8
UP, DOWN = 2.0**50, 2.0**-50


def pack(value):
    scaled = value * UP
    return (scaled * jnp.abs(scaled)).astype(BF16)


def unpack(code):
    code = code.astype(F32)
    return code * lax.rsqrt(jnp.maximum(jnp.abs(code), 2.0**-126)) * DOWN


def device(x, z, k, w, y):
    return ((x * 4 + z) * 2 + k, w * 4 + y)


def other(i):
    return i + 1 - 2 * (i % 2)


def kernel(
    r_ref, b_ref, yc, yp,
    rx, bf, part, acc, s1, r1, s2, r2, s3, r3, mid,
    b_sem, rx_send, rx_recv, rs_send, rs_recv, ag_send, ag_recv, fw_send, fw_recv, pn_send, pn_recv,
):
    t, c = lax.axis_index("tok"), lax.axis_index("col")
    x, z, k, w, y = t // 8, (t // 2) % 4, t % 2, c // 4, c % 4
    core = device(x, z, 1 - k, w, y)
    pair = device(x, z, k, 1 - w, y)
    diag = device(x, z, 1 - k, 1 - w, y)
    y_peers = {d: device(x, z, k, w, (y + d) % 4) for d in (1, 2, 3)}
    y_cores = {d: device(x, z, 1 - k, w, (y + d) % 4) for d in (1, 2, 3)}

    def along(x_axis, i):
        return device(i, z, k, w, y) if x_axis else device(x, i, k, w, y)

    x_peers = {d: along(True, (x + d) % 4) for d in (1, 2, 3)}
    z_peers = {d: along(False, (z + d) % 4) for d in (1, 2, 3)}
    mid_y = (z + y + 1) % 4
    panel_mid = device(x, z, w, k, mid_y)
    mid_self = (k == w) * (z == 3)
    via_y = (y - z - 1) % 4
    panel_back = device(x, z, w, k, via_y)
    to_x, to_z, to_k = 2 * k + via_y // 2, 2 * (via_y % 2) + x // 2, x % 2
    panel_to = device(to_x, to_z, to_k, w, y)
    to_self = (to_x == x) * (to_z == z) * (to_k == k)
    src_w, src_y = x // 2, (x % 2) * 2 + z // 2
    src_z = (y - src_y - 1) % 4
    panel_from = device((z % 2) * 2 + k, src_z, src_w, w, y)
    sends, sends_unless = [], []

    def remote(src, dst, send, recv, to):
        return pltpu.make_async_remote_copy(
            src_ref=src, dst_ref=dst, send_sem=send, recv_sem=recv, device_id=to, device_id_type=MESH
        )

    def start(*args):
        copy = remote(*args)
        copy.start()
        sends.append(copy)

    def start_unless(here, src, dst, send, recv, to):
        copy = remote(src, dst, send, recv, to)

        @pl.when(here)
        def _():
            pltpu.make_async_copy(src, dst, recv).start()

        @pl.when(jnp.logical_not(here))
        def _():
            copy.start()

        sends_unless.append((here, copy))

    def wait(dst, recv):
        remote(dst, dst, recv, recv, core).wait_recv()

    def group(block, core_index):
        place = (w + CROSS[block]) % 2 * 4 + (y + SHIFTS[block]) % 4
        return core_index * 8 + place

    own_rows = pl.ds(pl.multiple_of(k * 512, 512), 512)
    peer_rows = pl.ds(pl.multiple_of((1 - k) * 512, 512), 512)
    mine_r = r_ref.at[pl.ds(pl.multiple_of(k * 64, 64), 64), :]
    yours_r = r_ref.at[pl.ds(pl.multiple_of((1 - k) * 64, 64), 64), :]
    own_b = pltpu.make_async_copy(b_ref, bf.at[own_rows], b_sem.at[8])
    own_b.start()
    keep = pltpu.make_async_copy(mine_r, rx.at[0, :, own_rows], b_sem.at[9])
    keep.start()

    barrier = pltpu.get_barrier_semaphore()
    partners = [core, pair, diag, *y_peers.values(), *y_cores.values(), *x_peers.values(), *z_peers.values()]
    partners += [panel_mid, panel_back, panel_to, panel_from]
    for d in partners:
        pl.semaphore_signal(barrier, inc=1, device_id=d, device_id_type=MESH)
    pl.semaphore_wait(barrier, len(partners))

    def half_sem(block, whose):
        return rx_recv.at[2 * block + whose]

    sent = [0]

    def r_send(src, block, dst, to, whose=None):
        start(src, dst, rx_send.at[sent[0]], half_sem(block, k if whose is None else whose), to)
        sent[0] += 1

    r_send(yours_r, 0, rx.at[0, :, own_rows], core)
    r_send(mine_r, 1, rx.at[1, :, own_rows], pair)
    r_send(yours_r, 1, rx.at[1, :, own_rows], diag)
    for block, d in ((2, 2), (3, 1), (4, 3)):
        r_send(mine_r, block, rx.at[block, :, own_rows], y_peers[d])
        r_send(yours_r, block, rx.at[block, :, own_rows], y_cores[d])

    def roles(i, block, core_index):
        flip = (block + core_index) % 2
        p1 = other(i) * (1 - flip) + (3 - i) * flip
        return i, p1, other(i) + 3 - i - p1, (i + 2) % 4

    def order(block, core_index):
        me, p1, p2, opp = roles(x, block, core_index)
        return [opp, p1, p2, me]

    for i, o in enumerate(order(0, 1 - k)):
        cols = pl.ds(pl.multiple_of(o * 512, 512), 512)
        start(b_ref.at[:, cols], bf.at[own_rows, cols], b_sem.at[i], b_sem.at[4 + i], core)

    def hand_on(block):
        if block == 1:
            r_send(rx.at[1], 5, rx.at[5], y_peers[1], whose=0)
            r_send(rx.at[1], 6, rx.at[6], y_peers[3], whose=0)
        if block == 2:
            r_send(rx.at[2], 7, rx.at[7], pair, whose=0)

    def arrive(block):
        if block == 0:
            keep.wait()
            wait(rx.at[0, :, peer_rows], half_sem(0, 1 - k))
        elif block < 5:
            wait(rx.at[block, :, own_rows], half_sem(block, k))
            wait(rx.at[block, :, peer_rows], half_sem(block, 1 - k))
            hand_on(block)
        else:
            wait(rx.at[block], half_sem(block, 0))

    places = {True: x, False: z}

    def owned(block, first):
        return part.at[block, first] if X_FIRST[block] else part.at[block, :, first]

    def rs_sems(block, i):
        return rs_send.at[block * 6 + i], rs_recv.at[block * 6 + i]

    def first(block, slot, owner, p1):
        src, dst = (s1.at[block, slot], r1.at[block, slot]) if slot < 2 else (s2.at[block], r2.at[block])
        src[...] = pack(owned(block, owner)[...])
        start(src, dst, *rs_sems(block, slot), along(X_FIRST[block], p1))

    def dots(block):
        if block == 0:
            own_b.wait()
        me, p1, p2, opp = roles(places[X_FIRST[block]], block, k)
        for n, o in enumerate(order(block, k)):
            cols = pl.ds(pl.multiple_of(o * 512, 512), 512)
            if block == 0:
                wait(bf.at[peer_rows, cols], b_sem.at[4 + n])
            out = jnp.dot(rx[block], bf[:, cols], preferred_element_type=F32)
            for q in range(4):
                part[block, o, q] = out[:, q * 128 : (q + 1) * 128]
            if SUM_DIRECT[block]:
                if X_FIRST[block] and n < 3:
                    first(block, n, o, o)
            elif X_FIRST[block] and n < 2:
                first(block, n, o, p1)
        if SUM_DIRECT[block]:
            if not X_FIRST[block]:
                for n, o in enumerate((opp, p1, p2)):
                    first(block, n, o, o)
        elif not X_FIRST[block]:
            first(block, 0, opp, p1)
            first(block, 1, p1, p1)

    def second(block):
        if SUM_DIRECT[block]:
            return
        me, p1, p2, opp = roles(places[X_FIRST[block]], block, k)
        wait(r1.at[block, 0], rs_sems(block, 0)[1])
        s2[block] = pack(owned(block, p2)[...] + unpack(r1[block, 0]))
        start(s2.at[block], r2.at[block], *rs_sems(block, 2), along(X_FIRST[block], p2))

    def third(block):
        me = places[X_FIRST[block]]
        wait(r1.at[block, 1], rs_sems(block, 1)[1])
        wait(r2.at[block], rs_sems(block, 2)[1])
        total = owned(block, me)[...] + unpack(r1[block, 1]) + unpack(r2[block])
        if SUM_DIRECT[block]:
            wait(r1.at[block, 0], rs_sems(block, 0)[1])
            total += unpack(r1[block, 0])
        acc[block] = total
        i2 = places[not X_FIRST[block]]
        for n, d in enumerate((2, 1, 3)):
            to = (i2 + d) % 4
            s3[block, n] = pack(acc[block, to])
            start(s3.at[block, n], r3.at[block, n], *rs_sems(block, 3 + n), along(not X_FIRST[block], to))

    def ag_sems(block, i):
        return ag_send.at[block * 6 + i], ag_recv.at[block * 6 + i]

    def spot(block, core_index, inner, outer):
        g = group(block, core_index)
        a, b = (outer, inner) if X_FIRST[block] else (inner, outer)
        if b is None:
            return yc.at[g, a]
        return yc.at[g, :, b] if a is None else yc.at[g, a, b]

    def forward(block, i, ref):
        start(ref, ref, fw_send.at[block * 4 + i], fw_recv.at[block * 4 + i], core)

    def finish(block):
        i2 = places[not X_FIRST[block]]
        total = acc[block, i2]
        for n in range(3):
            wait(r3.at[block, n], rs_sems(block, 3 + n)[1])
            total += unpack(r3[block, n])
        g = group(block, k)
        yc[g, x, z] = total.astype(BF16)
        ref = yc.at[g, x, z]
        for n, d in enumerate((2, 1, 3)):
            start(ref, ref, *ag_sems(block, n), along(not X_FIRST[block], (i2 + d) % 4))
        start_unless(mid_self, ref, mid.at[block], *pn_sems(block, 8), panel_mid)

    def gather2(block):
        ii, oi = places[not X_FIRST[block]], places[X_FIRST[block]]
        me, p1, p2, opp = roles(oi, block, k)
        for n, d in enumerate((2, 1, 3)):
            wait(spot(block, k, (ii - d) % 4, oi), ag_sems(block, n)[1])
        ref = spot(block, k, None, oi)
        if GATHER_DIRECT[block]:
            start(ref, ref, *ag_sems(block, 5), along(X_FIRST[block], opp))
        start(ref, ref, *ag_sems(block, 3), along(X_FIRST[block], p1))
        start(ref, ref, *ag_sems(block, 4), along(X_FIRST[block], p2))
        forward(block, 0, ref)

    def gather3(block):
        me, p1, p2, opp = roles(places[X_FIRST[block]], block, k)
        ref = spot(block, k, None, p1)
        wait(ref, ag_sems(block, 3)[1])
        if not GATHER_DIRECT[block]:
            start(ref, ref, *ag_sems(block, 5), along(X_FIRST[block], p2))
        forward(block, 1, ref)

    def gather4(block):
        me, p1, p2, opp = roles(places[X_FIRST[block]], block, k)
        for n, o in ((4, p2), (5, opp)):
            ref = spot(block, k, None, o)
            wait(ref, ag_sems(block, n)[1])
            forward(block, n - 2, ref)

    def forwarded(block):
        for n, o in enumerate(roles(places[X_FIRST[block]], block, 1 - k)):
            wait(spot(block, 1 - k, None, o), fw_recv.at[block * 4 + n])

    def pn_sems(block, i):
        return pn_send.at[block * 9 + i], pn_recv.at[block * 9 + i]

    def panel_place(block, plane_w, plane_y, core_index):
        return core_index * 8 + (plane_w + CROSS[block]) % 2 * 4 + (plane_y + SHIFTS[block]) % 4

    def panel_spot(block, source, core_index):
        return yp.at[source, panel_place(block, src_w, src_y, core_index)]

    def panel1(block):
        wait(mid.at[block], pn_sems(block, 8)[1])
        ref = yp.at[z, panel_place(block, k, via_y, w)]
        start_unless(to_self, mid.at[block], ref, *pn_sems(block, 0), panel_to)

    def panel2(block):
        ref = panel_spot(block, src_z, w)
        wait(ref, pn_sems(block, 0)[1])
        start(ref, ref, *pn_sems(block, 1), pair)
        for n, d in enumerate((2, 1, 3)):
            start(ref, ref, *pn_sems(block, 2 + n), y_peers[d])

    def panel3(block):
        ref = panel_spot(block, src_z, 1 - w)
        wait(ref, pn_sems(block, 1)[1])
        for n, d in enumerate((2, 1, 3)):
            start(ref, ref, *pn_sems(block, 5 + n), y_peers[d])

    def panel4(block):
        for n, d in enumerate((2, 1, 3)):
            source = (y - d - src_y - 1) % 4
            wait(panel_spot(block, source, w), pn_sems(block, 2 + n)[1])
            wait(panel_spot(block, source, 1 - w), pn_sems(block, 5 + n)[1])

    plan = [
        (arrive, 0), (dots, 0), (arrive, 1), (dots, 1), (arrive, 2), (dots, 2), (second, 0), (arrive, 3), (dots, 3),
        (arrive, 4), (dots, 4), (arrive, 5), (dots, 5), (second, 1), (third, 0), (arrive, 6), (dots, 6),
        (arrive, 7), (dots, 7), (second, 2), (third, 1), (second, 4), (third, 2), (second, 5), (finish, 0),
        (second, 6), (second, 3), (second, 7), (third, 4), (finish, 1), (third, 5), (panel1, 0), (third, 6),
        (third, 7), (finish, 2), (gather2, 0), (third, 3), (finish, 4), (panel1, 1), (gather2, 1), (finish, 5),
        (panel1, 2), (finish, 6), (gather3, 0), (panel2, 0), (finish, 3), (finish, 7), (panel1, 4), (gather2, 2),
        (panel3, 0), (gather2, 4), (gather3, 1), (panel1, 5), (panel2, 1), (panel1, 6), (panel1, 3), (gather2, 3),
        (panel1, 7), (gather4, 0), (gather2, 5), (gather3, 2), (panel2, 2), (gather2, 6), (gather2, 7), (panel3, 1),
        (gather3, 4), (panel2, 4), (gather4, 1), (panel3, 2), (gather3, 5), (panel2, 5), (gather3, 6), (panel2, 6),
        (panel2, 3), (gather4, 2), (gather3, 3), (gather3, 7), (panel2, 7), (panel3, 4), (gather4, 4), (panel3, 5),
        (panel3, 6), (panel3, 3), (panel3, 7), (gather4, 5), (gather4, 6), (gather4, 7), (gather4, 3),
    ]
    for step, block in plan:
        step(block)
    for block in range(BLOCKS):
        panel4(block)
        forwarded(block)
    for copy in sends:
        copy.wait_send()
    for here, copy in sends_unless:
        pl.when(jnp.logical_not(here))(copy.wait_send)


def rotate(residual_rows, basis):
    dma = pltpu.SemaphoreType.DMA
    return pl.pallas_call(
        kernel,
        out_shape=[
            jax.ShapeDtypeStruct((16, 4, 4, 64, 128), BF16),
            jax.ShapeDtypeStruct((4, 16, 64, 128), BF16),
        ],
        in_specs=[pl.BlockSpec(memory_space=pltpu.VMEM), pl.BlockSpec(memory_space=pl.ANY)],
        out_specs=[pl.BlockSpec(memory_space=pltpu.VMEM)] * 2,
        scratch_shapes=[
            pltpu.VMEM((BLOCKS, 64, 1024), BF16),
            pltpu.VMEM((1024, 2048), BF16),
            pltpu.VMEM((BLOCKS, 4, 4, 64, 128), F32),
            pltpu.VMEM((BLOCKS, 4, 64, 128), F32),
            pltpu.VMEM((BLOCKS, 2, 4, 64, 128), BF16),
            pltpu.VMEM((BLOCKS, 2, 4, 64, 128), BF16),
            pltpu.VMEM((BLOCKS, 4, 64, 128), BF16),
            pltpu.VMEM((BLOCKS, 4, 64, 128), BF16),
            pltpu.VMEM((BLOCKS, 3, 64, 128), BF16),
            pltpu.VMEM((BLOCKS, 3, 64, 128), BF16),
            pltpu.VMEM((BLOCKS, 64, 128), BF16),
            dma((10,)),
            dma((12,)),
            dma((16,)),
            dma((BLOCKS * 6,)),
            dma((BLOCKS * 6,)),
            dma((BLOCKS * 6,)),
            dma((BLOCKS * 6,)),
            dma((BLOCKS * 4,)),
            dma((BLOCKS * 4,)),
            dma((BLOCKS * 9,)),
            dma((BLOCKS * 9,)),
        ],
        compiler_params=pltpu.CompilerParams(collective_id=0, has_side_effects=True, vmem_limit_bytes=28 * 2**20),
        cost_estimate=pl.CostEstimate(flops=2**31, bytes_accessed=8 * 2**20, transcendentals=0),
    )(residual_rows, basis)


def tile_kernel(columns, panel, tile, right, rows, sem):
    for n in range(4):
        right[:, n * 128 : (n + 1) * 128] = panel[n].reshape(1024, 128)
    copies = []
    for n in range(8):
        left = [columns[:, n // 2, n % 2 * 2 + q].reshape(1024, 128) for q in range(2)]
        out = lax.dot_general(
            jnp.concatenate(left, axis=1), right[...], (((0,), (0,)), ((), ())), preferred_element_type=F32
        )
        part = pl.ds(n * 256, 256)
        rows[part] = out * (1.0 / 1024)
        copies.append(pltpu.make_async_copy(rows.at[part], tile.at[part], sem.at[n]))
        copies[n].start()
    for copy in copies:
        copy.wait()


def body(residual_rows, basis):
    columns, panel = rotate(residual_rows, basis)
    return pl.pallas_call(
        tile_kernel,
        out_shape=jax.ShapeDtypeStruct((2048, 512), F32),
        in_specs=[pl.BlockSpec(memory_space=pltpu.VMEM)] * 2,
        out_specs=pl.BlockSpec(memory_space=pl.ANY),
        scratch_shapes=[
            pltpu.VMEM((1024, 512), BF16),
            pltpu.VMEM((2048, 512), F32),
            pltpu.SemaphoreType.DMA((8,)),
        ],
        compiler_params=pltpu.CompilerParams(vmem_limit_bytes=28 * 2**20),
        cost_estimate=pl.CostEstimate(flops=2**31, bytes_accessed=4 * 2**20, transcendentals=0),
    )(columns, panel)


def solution(mesh):
    return jax.shard_map(
        body,
        mesh=mesh,
        in_specs=(P("col", "tok"), P("tok", "col")),
        out_specs=P("col", "tok"),
        check_vma=False,
    )
```

```python
import jax
import jax.numpy as jnp
from jax import lax
from jax.experimental import pallas as pl
from jax.experimental.pallas import tpu as pltpu
from jax.sharding import PartitionSpec as P

MESH = pl.DeviceIdType.MESH
F32, BF16 = jnp.float32, jnp.bfloat16

SHIFTS = (0, 0, 2, 3, 1, 3, 1, 2)
CROSS = (0, 1, 0, 0, 0, 1, 1, 1)
X_FIRST = (True, True, False, True, True, True, True, True)
SUM_DIRECT = (False, False, False, False, False, False, False, False)
GATHER_DIRECT = (False, False, False, False, False, False, False, False)
SUM_HALVING = (False, False, False, False, False, False, False, False)
GATHER_HALVING = (True, True, True, True, True, True, True, True)
BLOCKS = 8
UP, DOWN = 2.0**50, 2.0**-50


def pack(value):
    scaled = value * UP
    return (scaled * jnp.abs(scaled)).astype(BF16)


def unpack(code):
    code = code.astype(F32)
    return code * lax.rsqrt(jnp.maximum(jnp.abs(code), 2.0**-126)) * DOWN


def device(x, z, k, w, y):
    return ((x * 4 + z) * 2 + k, w * 4 + y)


def other(i):
    return i + 1 - 2 * (i % 2)


def kernel(
    r_ref, b_ref, yc, yp,
    rx, bf, part, acc, s1, r1, s2, r2, s3, r3, mid,
    b_sem, rx_send, rx_recv, rs_send, rs_recv, ag_send, ag_recv, fw_send, fw_recv, pn_send, pn_recv,
):
    t, c = lax.axis_index("tok"), lax.axis_index("col")
    x, z, k, w, y = t // 8, (t // 2) % 4, t % 2, c // 4, c % 4
    core = device(x, z, 1 - k, w, y)
    pair = device(x, z, k, 1 - w, y)
    diag = device(x, z, 1 - k, 1 - w, y)
    y_peers = {d: device(x, z, k, w, (y + d) % 4) for d in (1, 2, 3)}
    y_cores = {d: device(x, z, 1 - k, w, (y + d) % 4) for d in (1, 2, 3)}

    def along(x_axis, i):
        return device(i, z, k, w, y) if x_axis else device(x, i, k, w, y)

    x_peers = {d: along(True, (x + d) % 4) for d in (1, 2, 3)}
    z_peers = {d: along(False, (z + d) % 4) for d in (1, 2, 3)}
    mid_y = (z + y + 1) % 4
    panel_mid = device(x, z, w, k, mid_y)
    mid_self = (k == w) * (z == 3)
    via_y = (y - z - 1) % 4
    panel_back = device(x, z, w, k, via_y)
    to_x, to_z, to_k = 2 * k + via_y // 2, 2 * (via_y % 2) + x // 2, x % 2
    panel_to = device(to_x, to_z, to_k, w, y)
    to_self = (to_x == x) * (to_z == z) * (to_k == k)
    src_w, src_y = x // 2, (x % 2) * 2 + z // 2
    src_z = (y - src_y - 1) % 4
    panel_from = device((z % 2) * 2 + k, src_z, src_w, w, y)
    sends, sends_unless = [], []

    def remote(src, dst, send, recv, to):
        return pltpu.make_async_remote_copy(
            src_ref=src, dst_ref=dst, send_sem=send, recv_sem=recv, device_id=to, device_id_type=MESH
        )

    def start(*args):
        copy = remote(*args)
        copy.start()
        sends.append(copy)

    def start_unless(here, src, dst, send, recv, to):
        copy = remote(src, dst, send, recv, to)

        @pl.when(here)
        def _():
            pltpu.make_async_copy(src, dst, recv).start()

        @pl.when(jnp.logical_not(here))
        def _():
            copy.start()

        sends_unless.append((here, copy))

    def wait(dst, recv):
        remote(dst, dst, recv, recv, core).wait_recv()

    def group(block, core_index):
        place = (w + CROSS[block]) % 2 * 4 + (y + SHIFTS[block]) % 4
        return core_index * 8 + place

    own_rows = pl.ds(pl.multiple_of(k * 512, 512), 512)
    peer_rows = pl.ds(pl.multiple_of((1 - k) * 512, 512), 512)
    mine_r = r_ref.at[pl.ds(pl.multiple_of(k * 64, 64), 64), :]
    yours_r = r_ref.at[pl.ds(pl.multiple_of((1 - k) * 64, 64), 64), :]
    own_b = pltpu.make_async_copy(b_ref, bf.at[own_rows], b_sem.at[8])
    own_b.start()
    keep = pltpu.make_async_copy(mine_r, rx.at[0, :, own_rows], b_sem.at[9])
    keep.start()

    barrier = pltpu.get_barrier_semaphore()
    partners = [core, pair, diag, *y_peers.values(), *y_cores.values(), *x_peers.values(), *z_peers.values()]
    partners += [panel_mid, panel_back, panel_to, panel_from]
    for d in partners:
        pl.semaphore_signal(barrier, inc=1, device_id=d, device_id_type=MESH)
    pl.semaphore_wait(barrier, len(partners))

    def half_sem(block, whose):
        return rx_recv.at[2 * block + whose]

    sent = [0]

    def r_send(src, block, dst, to, whose=None):
        start(src, dst, rx_send.at[sent[0]], half_sem(block, k if whose is None else whose), to)
        sent[0] += 1

    r_send(yours_r, 0, rx.at[0, :, own_rows], core)
    r_send(mine_r, 1, rx.at[1, :, own_rows], pair)
    r_send(yours_r, 1, rx.at[1, :, own_rows], diag)
    for block, d in ((2, 2), (3, 1), (4, 3)):
        r_send(mine_r, block, rx.at[block, :, own_rows], y_peers[d])
        r_send(yours_r, block, rx.at[block, :, own_rows], y_cores[d])

    def roles(i, block, core_index):
        flip = (block + core_index) % 2
        p1 = other(i) * (1 - flip) + (3 - i) * flip
        return i, p1, other(i) + 3 - i - p1, (i + 2) % 4

    def order(block, core_index):
        me, p1, p2, opp = roles(x, block, core_index)
        return [opp, p1, p2, me]

    for i, o in enumerate(order(0, 1 - k)):
        cols = pl.ds(pl.multiple_of(o * 512, 512), 512)
        start(b_ref.at[:, cols], bf.at[own_rows, cols], b_sem.at[i], b_sem.at[4 + i], core)

    def hand_on(block):
        if block == 1:
            r_send(rx.at[1], 5, rx.at[5], y_peers[1], whose=0)
            r_send(rx.at[1], 6, rx.at[6], y_peers[3], whose=0)
        if block == 2:
            r_send(rx.at[2], 7, rx.at[7], pair, whose=0)

    def arrive(block):
        if block == 0:
            keep.wait()
            wait(rx.at[0, :, peer_rows], half_sem(0, 1 - k))
        elif block < 5:
            wait(rx.at[block, :, own_rows], half_sem(block, k))
            wait(rx.at[block, :, peer_rows], half_sem(block, 1 - k))
            hand_on(block)
        else:
            wait(rx.at[block], half_sem(block, 0))

    places = {True: x, False: z}

    def owned(block, first):
        return part.at[block, first] if X_FIRST[block] else part.at[block, :, first]

    def rs_sems(block, i):
        return rs_send.at[block * 6 + i], rs_recv.at[block * 6 + i]

    def first(block, slot, owner, p1):
        src, dst = (s1.at[block, slot], r1.at[block, slot]) if slot < 2 else (s2.at[block], r2.at[block])
        src[...] = pack(owned(block, owner)[...])
        start(src, dst, *rs_sems(block, slot), along(X_FIRST[block], p1))

    def dots(block):
        if block == 0:
            own_b.wait()
        me, p1, p2, opp = roles(places[X_FIRST[block]], block, k)
        for n, o in enumerate(order(block, k)):
            cols = pl.ds(pl.multiple_of(o * 512, 512), 512)
            if block == 0:
                wait(bf.at[peer_rows, cols], b_sem.at[4 + n])
            out = jnp.dot(rx[block], bf[:, cols], preferred_element_type=F32)
            for q in range(4):
                part[block, o, q] = out[:, q * 128 : (q + 1) * 128]
            if SUM_DIRECT[block]:
                if X_FIRST[block] and n < 3:
                    first(block, n, o, o)
            elif X_FIRST[block] and n < 2:
                first(block, n, o, p1)
        if SUM_DIRECT[block]:
            if not X_FIRST[block]:
                for n, o in enumerate((opp, p1, p2)):
                    first(block, n, o, o)
        elif not X_FIRST[block]:
            first(block, 0, opp, p1)
            first(block, 1, p1, p1)

    def second(block):
        if SUM_DIRECT[block]:
            return
        me, p1, p2, opp = roles(places[X_FIRST[block]], block, k)
        wait(r1.at[block, 0], rs_sems(block, 0)[1])
        s2[block] = pack(owned(block, p2)[...] + unpack(r1[block, 0]))
        start(s2.at[block], r2.at[block], *rs_sems(block, 2), along(X_FIRST[block], p2))

    def third(block):
        me = places[X_FIRST[block]]
        wait(r1.at[block, 1], rs_sems(block, 1)[1])
        wait(r2.at[block], rs_sems(block, 2)[1])
        total = owned(block, me)[...] + unpack(r1[block, 1]) + unpack(r2[block])
        if SUM_DIRECT[block]:
            wait(r1.at[block, 0], rs_sems(block, 0)[1])
            total += unpack(r1[block, 0])
        acc[block] = total
        i2 = places[not X_FIRST[block]]
        if SUM_HALVING[block]:
            me, p1, p2, opp = roles(i2, block, k)
            for n, to in enumerate((opp, p1)):
                s3[block, n] = pack(acc[block, to])
                start(s3.at[block, n], r3.at[block, n], *rs_sems(block, 3 + n), along(not X_FIRST[block], p1))
            return
        for n, d in enumerate((2, 1, 3)):
            to = (i2 + d) % 4
            s3[block, n] = pack(acc[block, to])
            start(s3.at[block, n], r3.at[block, n], *rs_sems(block, 3 + n), along(not X_FIRST[block], to))

    def fourth(block):
        if not SUM_HALVING[block]:
            return
        me, p1, p2, opp = roles(places[not X_FIRST[block]], block, k)
        wait(r3.at[block, 0], rs_sems(block, 3)[1])
        s3[block, 2] = pack(acc[block, p2] + unpack(r3[block, 0]))
        start(s3.at[block, 2], r3.at[block, 2], *rs_sems(block, 5), along(not X_FIRST[block], p2))

    def ag_sems(block, i):
        return ag_send.at[block * 6 + i], ag_recv.at[block * 6 + i]

    def spot(block, core_index, inner, outer):
        g = group(block, core_index)
        a, b = (outer, inner) if X_FIRST[block] else (inner, outer)
        if b is None:
            return yc.at[g, a]
        return yc.at[g, :, b] if a is None else yc.at[g, a, b]

    def forward(block, i, ref):
        start(ref, ref, fw_send.at[block * 4 + i], fw_recv.at[block * 4 + i], core)

    def finish(block):
        i2 = places[not X_FIRST[block]]
        total = acc[block, i2]
        for n in range(1 if SUM_HALVING[block] else 0, 3):
            wait(r3.at[block, n], rs_sems(block, 3 + n)[1])
            total += unpack(r3[block, n])
        g = group(block, k)
        yc[g, x, z] = total.astype(BF16)
        ref = yc.at[g, x, z]
        if GATHER_HALVING[block]:
            me, p1, p2, opp = roles(i2, block, k)
            start(ref, ref, *ag_sems(block, 0), along(not X_FIRST[block], p1))
            start(ref, ref, *ag_sems(block, 1), along(not X_FIRST[block], p2))
        else:
            for n, d in enumerate((2, 1, 3)):
                start(ref, ref, *ag_sems(block, n), along(not X_FIRST[block], (i2 + d) % 4))
        start_unless(mid_self, ref, mid.at[block], *pn_sems(block, 8), panel_mid)

    def gather1(block):
        if not GATHER_HALVING[block]:
            return
        ii, oi = places[not X_FIRST[block]], places[X_FIRST[block]]
        me, p1, p2, opp = roles(ii, block, k)
        ref = spot(block, k, p1, oi)
        wait(ref, ag_sems(block, 0)[1])
        start(ref, ref, *ag_sems(block, 2), along(not X_FIRST[block], p2))

    def gather2(block):
        ii, oi = places[not X_FIRST[block]], places[X_FIRST[block]]
        me, p1, p2, opp = roles(oi, block, k)
        if GATHER_HALVING[block]:
            me, p1, p2, opp = roles(ii, block, k)
            wait(spot(block, k, p2, oi), ag_sems(block, 1)[1])
            wait(spot(block, k, opp, oi), ag_sems(block, 2)[1])
        else:
            for n, d in enumerate((2, 1, 3)):
                wait(spot(block, k, (ii - d) % 4, oi), ag_sems(block, n)[1])
        me, p1, p2, opp = roles(oi, block, k)
        ref = spot(block, k, None, oi)
        if GATHER_DIRECT[block]:
            start(ref, ref, *ag_sems(block, 5), along(X_FIRST[block], opp))
        start(ref, ref, *ag_sems(block, 3), along(X_FIRST[block], p1))
        start(ref, ref, *ag_sems(block, 4), along(X_FIRST[block], p2))
        forward(block, 0, ref)

    def gather3(block):
        me, p1, p2, opp = roles(places[X_FIRST[block]], block, k)
        ref = spot(block, k, None, p1)
        wait(ref, ag_sems(block, 3)[1])
        if not GATHER_DIRECT[block]:
            start(ref, ref, *ag_sems(block, 5), along(X_FIRST[block], p2))
        forward(block, 1, ref)

    def gather4(block):
        me, p1, p2, opp = roles(places[X_FIRST[block]], block, k)
        for n, o in ((4, p2), (5, opp)):
            ref = spot(block, k, None, o)
            wait(ref, ag_sems(block, n)[1])
            forward(block, n - 2, ref)

    def forwarded(block):
        for n, o in enumerate(roles(places[X_FIRST[block]], block, 1 - k)):
            wait(spot(block, 1 - k, None, o), fw_recv.at[block * 4 + n])

    def pn_sems(block, i):
        return pn_send.at[block * 9 + i], pn_recv.at[block * 9 + i]

    def panel_place(block, plane_w, plane_y, core_index):
        return core_index * 8 + (plane_w + CROSS[block]) % 2 * 4 + (plane_y + SHIFTS[block]) % 4

    def panel_spot(block, source, core_index):
        return yp.at[source, panel_place(block, src_w, src_y, core_index)]

    def panel1(block):
        wait(mid.at[block], pn_sems(block, 8)[1])
        ref = yp.at[z, panel_place(block, k, via_y, w)]
        start_unless(to_self, mid.at[block], ref, *pn_sems(block, 0), panel_to)

    def panel2(block):
        ref = panel_spot(block, src_z, w)
        wait(ref, pn_sems(block, 0)[1])
        start(ref, ref, *pn_sems(block, 1), pair)
        for n, d in enumerate((2, 1, 3)):
            start(ref, ref, *pn_sems(block, 2 + n), y_peers[d])

    def panel3(block):
        ref = panel_spot(block, src_z, 1 - w)
        wait(ref, pn_sems(block, 1)[1])
        for n, d in enumerate((2, 1, 3)):
            start(ref, ref, *pn_sems(block, 5 + n), y_peers[d])

    def panel4(block):
        for n, d in enumerate((2, 1, 3)):
            source = (y - d - src_y - 1) % 4
            wait(panel_spot(block, source, w), pn_sems(block, 2 + n)[1])
            wait(panel_spot(block, source, 1 - w), pn_sems(block, 5 + n)[1])

    plan = [
        (arrive, 0), (dots, 0), (arrive, 1), (dots, 1), (arrive, 2), (dots, 2), (second, 0), (arrive, 3), (dots, 3),
        (arrive, 4), (dots, 4), (arrive, 5), (dots, 5), (second, 1), (third, 0), (arrive, 6), (dots, 6),
        (arrive, 7), (dots, 7), (second, 3), (third, 1), (second, 4), (second, 2), (second, 5), (finish, 0),
        (second, 6), (second, 7), (third, 3), (third, 4), (finish, 1), (third, 5), (gather1, 0), (panel1, 0),
        (third, 6), (third, 7), (third, 2), (finish, 3), (gather1, 1), (finish, 4), (panel1, 1), (gather2, 0),
        (panel2, 0), (finish, 2), (finish, 5), (finish, 6), (finish, 7), (gather1, 3), (panel1, 3), (gather1, 4),
        (gather2, 1), (panel1, 4), (panel3, 0), (gather1, 2), (gather3, 0), (panel2, 1), (panel1, 2), (gather1, 5),
        (panel1, 5), (gather1, 6), (panel1, 6), (gather1, 7), (panel1, 7), (gather2, 2), (gather2, 3), (panel3, 1),
        (gather2, 4), (gather3, 1), (panel2, 3), (panel2, 4), (gather4, 0), (gather2, 5), (panel2, 2), (gather2, 6),
        (gather2, 7), (panel2, 5), (panel3, 3), (gather3, 3), (panel2, 6), (panel3, 4), (gather3, 4), (panel2, 7),
        (gather4, 1), (panel3, 2), (gather3, 2), (panel3, 5), (panel3, 6), (gather3, 5), (panel3, 7), (gather3, 6),
        (gather3, 7), (gather4, 3), (gather4, 4), (gather4, 5), (gather4, 6), (gather4, 7), (gather4, 2),
    ]
    for step, block in plan:
        step(block)
    for block in range(BLOCKS):
        panel4(block)
        forwarded(block)
    for copy in sends:
        copy.wait_send()
    for here, copy in sends_unless:
        pl.when(jnp.logical_not(here))(copy.wait_send)


def rotate(residual_rows, basis):
    dma = pltpu.SemaphoreType.DMA
    return pl.pallas_call(
        kernel,
        out_shape=[
            jax.ShapeDtypeStruct((16, 4, 4, 64, 128), BF16),
            jax.ShapeDtypeStruct((4, 16, 64, 128), BF16),
        ],
        in_specs=[pl.BlockSpec(memory_space=pltpu.VMEM), pl.BlockSpec(memory_space=pl.ANY)],
        out_specs=[pl.BlockSpec(memory_space=pltpu.VMEM)] * 2,
        scratch_shapes=[
            pltpu.VMEM((BLOCKS, 64, 1024), BF16),
            pltpu.VMEM((1024, 2048), BF16),
            pltpu.VMEM((BLOCKS, 4, 4, 64, 128), F32),
            pltpu.VMEM((BLOCKS, 4, 64, 128), F32),
            pltpu.VMEM((BLOCKS, 2, 4, 64, 128), BF16),
            pltpu.VMEM((BLOCKS, 2, 4, 64, 128), BF16),
            pltpu.VMEM((BLOCKS, 4, 64, 128), BF16),
            pltpu.VMEM((BLOCKS, 4, 64, 128), BF16),
            pltpu.VMEM((BLOCKS, 3, 64, 128), BF16),
            pltpu.VMEM((BLOCKS, 3, 64, 128), BF16),
            pltpu.VMEM((BLOCKS, 64, 128), BF16),
            dma((10,)),
            dma((12,)),
            dma((16,)),
            dma((BLOCKS * 6,)),
            dma((BLOCKS * 6,)),
            dma((BLOCKS * 6,)),
            dma((BLOCKS * 6,)),
            dma((BLOCKS * 4,)),
            dma((BLOCKS * 4,)),
            dma((BLOCKS * 9,)),
            dma((BLOCKS * 9,)),
        ],
        compiler_params=pltpu.CompilerParams(collective_id=0, has_side_effects=True, vmem_limit_bytes=28 * 2**20),
        cost_estimate=pl.CostEstimate(flops=2**31, bytes_accessed=8 * 2**20, transcendentals=0),
    )(residual_rows, basis)


def tile_kernel(columns, panel, tile, right, rows, sem):
    for n in range(4):
        right[:, n * 128 : (n + 1) * 128] = panel[n].reshape(1024, 128)
    copies = []
    for n in range(8):
        left = [columns[:, n // 2, n % 2 * 2 + q].reshape(1024, 128) for q in range(2)]
        out = lax.dot_general(
            jnp.concatenate(left, axis=1), right[...], (((0,), (0,)), ((), ())), preferred_element_type=F32
        )
        part = pl.ds(n * 256, 256)
        rows[part] = out * (1.0 / 1024)
        copies.append(pltpu.make_async_copy(rows.at[part], tile.at[part], sem.at[n]))
        copies[n].start()
    for copy in copies:
        copy.wait()


def body(residual_rows, basis):
    columns, panel = rotate(residual_rows, basis)
    return pl.pallas_call(
        tile_kernel,
        out_shape=jax.ShapeDtypeStruct((2048, 512), F32),
        in_specs=[pl.BlockSpec(memory_space=pltpu.VMEM)] * 2,
        out_specs=pl.BlockSpec(memory_space=pl.ANY),
        scratch_shapes=[
            pltpu.VMEM((1024, 512), BF16),
            pltpu.VMEM((2048, 512), F32),
            pltpu.SemaphoreType.DMA((8,)),
        ],
        compiler_params=pltpu.CompilerParams(vmem_limit_bytes=28 * 2**20),
        cost_estimate=pl.CostEstimate(flops=2**31, bytes_accessed=4 * 2**20, transcendentals=0),
    )(columns, panel)


def solution(mesh):
    return jax.shard_map(
        body,
        mesh=mesh,
        in_specs=(P("col", "tok"), P("tok", "col")),
        out_specs=P("col", "tok"),
        check_vma=False,
    )
```

```python
import jax
import jax.numpy as jnp
from jax import lax
from jax.experimental import pallas as pl
from jax.experimental.pallas import tpu as pltpu
from jax.sharding import PartitionSpec as P

MESH = pl.DeviceIdType.MESH
F32, BF16 = jnp.float32, jnp.bfloat16

SHIFTS = (0, 0, 2, 3, 1, 3, 1, 2)
CROSS = (0, 1, 0, 0, 0, 1, 1, 1)
X_FIRST = (True, True, False, True, True, True, True, True)
SUM_DIRECT = (False, False, False, False, False, False, False, False)
GATHER_DIRECT = (False, False, False, False, False, False, False, False)
SUM_HALVING = (False, False, False, False, False, False, False, False)
GATHER_HALVING = (True, True, True, True, True, True, True, True)
BLOCKS = 8
UP, DOWN = 2.0**50, 2.0**-50


def pack(value):
    scaled = value * UP
    return (scaled * jnp.abs(scaled)).astype(BF16)


def unpack(code):
    code = code.astype(F32)
    return code * lax.rsqrt(jnp.maximum(jnp.abs(code), 2.0**-126)) * DOWN


def device(x, z, k, w, y):
    return ((x * 4 + z) * 2 + k, w * 4 + y)


def other(i):
    return i + 1 - 2 * (i % 2)


def kernel(
    r_ref, b_ref, yc, yp,
    rx, bf, part, acc, s1, r1, s2, r2, s3, r3, mid,
    b_sem, rx_send, rx_recv, rs_send, rs_recv, ag_send, ag_recv, fw_send, fw_recv, pn_send, pn_recv,
):
    t, c = lax.axis_index("tok"), lax.axis_index("col")
    x, z, k, w, y = t // 8, (t // 2) % 4, t % 2, c // 4, c % 4
    core = device(x, z, 1 - k, w, y)
    pair = device(x, z, k, 1 - w, y)
    diag = device(x, z, 1 - k, 1 - w, y)
    y_peers = {d: device(x, z, k, w, (y + d) % 4) for d in (1, 2, 3)}
    y_cores = {d: device(x, z, 1 - k, w, (y + d) % 4) for d in (1, 2, 3)}

    def along(x_axis, i):
        return device(i, z, k, w, y) if x_axis else device(x, i, k, w, y)

    x_peers = {d: along(True, (x + d) % 4) for d in (1, 2, 3)}
    z_peers = {d: along(False, (z + d) % 4) for d in (1, 2, 3)}
    mid_y = (z + y + 1) % 4
    panel_mid = device(x, z, w, k, mid_y)
    mid_self = (k == w) * (z == 3)
    via_y = (y - z - 1) % 4
    panel_back = device(x, z, w, k, via_y)
    to_x, to_z, to_k = 2 * k + via_y // 2, 2 * (via_y % 2) + x // 2, x % 2
    panel_to = device(to_x, to_z, to_k, w, y)
    to_self = (to_x == x) * (to_z == z) * (to_k == k)
    src_w, src_y = x // 2, (x % 2) * 2 + z // 2
    src_z = (y - src_y - 1) % 4
    panel_from = device((z % 2) * 2 + k, src_z, src_w, w, y)
    sends, sends_unless = [], []

    def remote(src, dst, send, recv, to):
        return pltpu.make_async_remote_copy(
            src_ref=src, dst_ref=dst, send_sem=send, recv_sem=recv, device_id=to, device_id_type=MESH
        )

    def start(*args):
        copy = remote(*args)
        copy.start()
        sends.append(copy)

    def start_unless(here, src, dst, send, recv, to):
        copy = remote(src, dst, send, recv, to)

        @pl.when(here)
        def _():
            pltpu.make_async_copy(src, dst, recv).start()

        @pl.when(jnp.logical_not(here))
        def _():
            copy.start()

        sends_unless.append((here, copy))

    def wait(dst, recv):
        remote(dst, dst, recv, recv, core).wait_recv()

    def group(block, core_index):
        place = (w + CROSS[block]) % 2 * 4 + (y + SHIFTS[block]) % 4
        return core_index * 8 + place

    own_rows = pl.ds(pl.multiple_of(k * 512, 512), 512)
    peer_rows = pl.ds(pl.multiple_of((1 - k) * 512, 512), 512)
    mine_r = r_ref.at[pl.ds(pl.multiple_of(k * 64, 64), 64), :]
    yours_r = r_ref.at[pl.ds(pl.multiple_of((1 - k) * 64, 64), 64), :]
    own_b = pltpu.make_async_copy(b_ref, bf.at[own_rows], b_sem.at[8])
    own_b.start()
    keep = pltpu.make_async_copy(mine_r, rx.at[0, :, own_rows], b_sem.at[9])
    keep.start()

    barrier = pltpu.get_barrier_semaphore()
    partners = [core, pair, diag, *y_peers.values(), *y_cores.values(), *x_peers.values(), *z_peers.values()]
    partners += [panel_mid, panel_back, panel_to, panel_from]
    for d in partners:
        pl.semaphore_signal(barrier, inc=1, device_id=d, device_id_type=MESH)
    pl.semaphore_wait(barrier, len(partners))

    def half_sem(block, whose):
        return rx_recv.at[2 * block + whose]

    sent = [0]

    def r_send(src, block, dst, to, whose=None):
        start(src, dst, rx_send.at[sent[0]], half_sem(block, k if whose is None else whose), to)
        sent[0] += 1

    r_send(yours_r, 0, rx.at[0, :, own_rows], core)
    r_send(mine_r, 1, rx.at[1, :, own_rows], pair)
    r_send(yours_r, 1, rx.at[1, :, own_rows], diag)
    for block, d in ((2, 2), (3, 1), (4, 3)):
        r_send(mine_r, block, rx.at[block, :, own_rows], y_peers[d])
        r_send(yours_r, block, rx.at[block, :, own_rows], y_cores[d])

    def roles(i, block, core_index):
        flip = (block + core_index) % 2
        p1 = other(i) * (1 - flip) + (3 - i) * flip
        return i, p1, other(i) + 3 - i - p1, (i + 2) % 4

    def order(block, core_index):
        me, p1, p2, opp = roles(x, block, core_index)
        return [opp, p1, p2, me]

    for i, o in enumerate(order(0, 1 - k)):
        cols = pl.ds(pl.multiple_of(o * 512, 512), 512)
        start(b_ref.at[:, cols], bf.at[own_rows, cols], b_sem.at[i], b_sem.at[4 + i], core)

    def hand_on(block):
        if block == 1:
            r_send(rx.at[1], 5, rx.at[5], y_peers[1], whose=0)
            r_send(rx.at[1], 6, rx.at[6], y_peers[3], whose=0)
        if block == 2:
            r_send(rx.at[2], 7, rx.at[7], pair, whose=0)

    def arrive(block):
        if block == 0:
            keep.wait()
            wait(rx.at[0, :, peer_rows], half_sem(0, 1 - k))
        elif block < 5:
            wait(rx.at[block, :, own_rows], half_sem(block, k))
            wait(rx.at[block, :, peer_rows], half_sem(block, 1 - k))
            hand_on(block)
        else:
            wait(rx.at[block], half_sem(block, 0))

    places = {True: x, False: z}

    def owned(block, first):
        return part.at[block, first] if X_FIRST[block] else part.at[block, :, first]

    def rs_sems(block, i):
        return rs_send.at[block * 6 + i], rs_recv.at[block * 6 + i]

    def first(block, slot, owner, p1):
        src, dst = (s1.at[block, slot], r1.at[block, slot]) if slot < 2 else (s2.at[block], r2.at[block])
        src[...] = pack(owned(block, owner)[...])
        start(src, dst, *rs_sems(block, slot), along(X_FIRST[block], p1))

    def dots(block):
        if block == 0:
            own_b.wait()
        me, p1, p2, opp = roles(places[X_FIRST[block]], block, k)
        for n, o in enumerate(order(block, k)):
            cols = pl.ds(pl.multiple_of(o * 512, 512), 512)
            if block == 0:
                wait(bf.at[peer_rows, cols], b_sem.at[4 + n])
            out = jnp.dot(rx[block], bf[:, cols], preferred_element_type=F32)
            for q in range(4):
                part[block, o, q] = out[:, q * 128 : (q + 1) * 128]
            if SUM_DIRECT[block]:
                if X_FIRST[block] and n < 3:
                    first(block, n, o, o)
            elif X_FIRST[block] and n < 2:
                first(block, n, o, p1)
        if SUM_DIRECT[block]:
            if not X_FIRST[block]:
                for n, o in enumerate((opp, p1, p2)):
                    first(block, n, o, o)
        elif not X_FIRST[block]:
            first(block, 0, opp, p1)
            first(block, 1, p1, p1)

    def second(block):
        if SUM_DIRECT[block]:
            return
        me, p1, p2, opp = roles(places[X_FIRST[block]], block, k)
        wait(r1.at[block, 0], rs_sems(block, 0)[1])
        s2[block] = pack(owned(block, p2)[...] + unpack(r1[block, 0]))
        start(s2.at[block], r2.at[block], *rs_sems(block, 2), along(X_FIRST[block], p2))

    def third(block):
        me = places[X_FIRST[block]]
        wait(r1.at[block, 1], rs_sems(block, 1)[1])
        wait(r2.at[block], rs_sems(block, 2)[1])
        total = owned(block, me)[...] + unpack(r1[block, 1]) + unpack(r2[block])
        if SUM_DIRECT[block]:
            wait(r1.at[block, 0], rs_sems(block, 0)[1])
            total += unpack(r1[block, 0])
        acc[block] = total
        i2 = places[not X_FIRST[block]]
        if SUM_HALVING[block]:
            me, p1, p2, opp = roles(i2, block, k)
            for n, to in enumerate((opp, p1)):
                s3[block, n] = pack(acc[block, to])
                start(s3.at[block, n], r3.at[block, n], *rs_sems(block, 3 + n), along(not X_FIRST[block], p1))
            return
        for n, d in enumerate((2, 1, 3)):
            to = (i2 + d) % 4
            s3[block, n] = pack(acc[block, to])
            start(s3.at[block, n], r3.at[block, n], *rs_sems(block, 3 + n), along(not X_FIRST[block], to))

    def fourth(block):
        if not SUM_HALVING[block]:
            return
        me, p1, p2, opp = roles(places[not X_FIRST[block]], block, k)
        wait(r3.at[block, 0], rs_sems(block, 3)[1])
        s3[block, 2] = pack(acc[block, p2] + unpack(r3[block, 0]))
        start(s3.at[block, 2], r3.at[block, 2], *rs_sems(block, 5), along(not X_FIRST[block], p2))

    def ag_sems(block, i):
        return ag_send.at[block * 6 + i], ag_recv.at[block * 6 + i]

    def spot(block, core_index, inner, outer):
        g = group(block, core_index)
        a, b = (outer, inner) if X_FIRST[block] else (inner, outer)
        if b is None:
            return yc.at[g, a]
        return yc.at[g, :, b] if a is None else yc.at[g, a, b]

    def forward(block, i, ref):
        start(ref, ref, fw_send.at[block * 4 + i], fw_recv.at[block * 4 + i], core)

    def finish(block):
        i2 = places[not X_FIRST[block]]
        total = acc[block, i2]
        for n in range(1 if SUM_HALVING[block] else 0, 3):
            wait(r3.at[block, n], rs_sems(block, 3 + n)[1])
            total += unpack(r3[block, n])
        g = group(block, k)
        yc[g, x, z] = total.astype(BF16)
        ref = yc.at[g, x, z]
        if GATHER_HALVING[block]:
            me, p1, p2, opp = roles(i2, block, k)
            start(ref, ref, *ag_sems(block, 0), along(not X_FIRST[block], p1))
            start(ref, ref, *ag_sems(block, 1), along(not X_FIRST[block], p2))
        else:
            for n, d in enumerate((2, 1, 3)):
                start(ref, ref, *ag_sems(block, n), along(not X_FIRST[block], (i2 + d) % 4))
        start_unless(mid_self, ref, mid.at[block], *pn_sems(block, 8), panel_mid)

    def gather1(block):
        if not GATHER_HALVING[block]:
            return
        ii, oi = places[not X_FIRST[block]], places[X_FIRST[block]]
        me, p1, p2, opp = roles(ii, block, k)
        ref = spot(block, k, p1, oi)
        wait(ref, ag_sems(block, 0)[1])
        start(ref, ref, *ag_sems(block, 2), along(not X_FIRST[block], p2))

    def gather2(block):
        ii, oi = places[not X_FIRST[block]], places[X_FIRST[block]]
        me, p1, p2, opp = roles(oi, block, k)
        if GATHER_HALVING[block]:
            me, p1, p2, opp = roles(ii, block, k)
            wait(spot(block, k, p2, oi), ag_sems(block, 1)[1])
            wait(spot(block, k, opp, oi), ag_sems(block, 2)[1])
        else:
            for n, d in enumerate((2, 1, 3)):
                wait(spot(block, k, (ii - d) % 4, oi), ag_sems(block, n)[1])
        me, p1, p2, opp = roles(oi, block, k)
        ref = spot(block, k, None, oi)
        if GATHER_DIRECT[block]:
            start(ref, ref, *ag_sems(block, 5), along(X_FIRST[block], opp))
        start(ref, ref, *ag_sems(block, 3), along(X_FIRST[block], p1))
        start(ref, ref, *ag_sems(block, 4), along(X_FIRST[block], p2))
        forward(block, 0, ref)

    def gather3(block):
        me, p1, p2, opp = roles(places[X_FIRST[block]], block, k)
        ref = spot(block, k, None, p1)
        wait(ref, ag_sems(block, 3)[1])
        if not GATHER_DIRECT[block]:
            start(ref, ref, *ag_sems(block, 5), along(X_FIRST[block], p2))
        forward(block, 1, ref)

    def gather4(block):
        me, p1, p2, opp = roles(places[X_FIRST[block]], block, k)
        for n, o in ((4, p2), (5, opp)):
            ref = spot(block, k, None, o)
            wait(ref, ag_sems(block, n)[1])
            forward(block, n - 2, ref)

    def forwarded(block):
        for n, o in enumerate(roles(places[X_FIRST[block]], block, 1 - k)):
            wait(spot(block, 1 - k, None, o), fw_recv.at[block * 4 + n])

    def pn_sems(block, i):
        return pn_send.at[block * 9 + i], pn_recv.at[block * 9 + i]

    def panel_place(block, plane_w, plane_y, core_index):
        return core_index * 8 + (plane_w + CROSS[block]) % 2 * 4 + (plane_y + SHIFTS[block]) % 4

    def panel_spot(block, source, core_index):
        return yp.at[source, panel_place(block, src_w, src_y, core_index)]

    def panel1(block):
        wait(mid.at[block], pn_sems(block, 8)[1])
        ref = yp.at[z, panel_place(block, k, via_y, w)]
        start_unless(to_self, mid.at[block], ref, *pn_sems(block, 0), panel_to)

    def panel2(block):
        ref = panel_spot(block, src_z, w)
        wait(ref, pn_sems(block, 0)[1])
        start(ref, ref, *pn_sems(block, 1), pair)
        for n, d in enumerate((2, 1, 3)):
            start(ref, ref, *pn_sems(block, 2 + n), y_peers[d])

    def panel3(block):
        ref = panel_spot(block, src_z, 1 - w)
        wait(ref, pn_sems(block, 1)[1])
        for n, d in enumerate((2, 1, 3)):
            start(ref, ref, *pn_sems(block, 5 + n), y_peers[d])

    def panel4(block):
        for n, d in enumerate((2, 1, 3)):
            source = (y - d - src_y - 1) % 4
            wait(panel_spot(block, source, w), pn_sems(block, 2 + n)[1])
            wait(panel_spot(block, source, 1 - w), pn_sems(block, 5 + n)[1])

    plan = [
        (arrive, 0), (dots, 0), (arrive, 1), (dots, 1), (arrive, 2), (dots, 2), (second, 0), (arrive, 3), (dots, 3),
        (arrive, 4), (dots, 4), (arrive, 5), (dots, 5), (second, 1), (third, 0), (arrive, 6), (dots, 6),
        (arrive, 7), (dots, 7), (second, 3), (third, 1), (second, 4), (second, 2), (second, 5), (finish, 0),
        (second, 6), (second, 7), (third, 3), (third, 4), (finish, 1), (third, 5), (gather1, 0), (third, 6),
        (third, 7), (third, 2), (panel1, 0), (finish, 3), (gather1, 1), (finish, 4), (gather2, 0), (panel1, 1),
        (finish, 2), (finish, 5), (finish, 6), (finish, 7), (panel2, 0), (gather1, 3), (gather1, 4), (gather2, 1),
        (gather1, 2), (gather3, 0), (panel1, 3), (panel1, 4), (gather1, 5), (panel3, 0), (panel1, 2), (gather1, 6),
        (panel2, 1), (gather1, 7), (panel1, 5), (gather2, 2), (gather2, 3), (panel1, 6), (gather2, 4), (gather3, 1),
        (panel1, 7), (gather4, 0), (panel3, 1), (gather2, 5), (panel2, 3), (gather2, 6), (panel2, 4), (gather2, 7),
        (gather3, 3), (gather3, 4), (panel2, 2), (gather4, 1), (panel2, 5), (panel2, 6), (panel3, 3), (gather3, 2),
        (panel2, 7), (panel3, 4), (gather3, 5), (gather3, 6), (gather3, 7), (panel3, 2), (panel3, 5), (gather4, 3),
        (panel3, 6), (gather4, 4), (panel3, 7), (gather4, 5), (gather4, 6), (gather4, 7), (gather4, 2),
    ]
    for step, block in plan:
        step(block)
    for block in range(BLOCKS):
        panel4(block)
        forwarded(block)
    for copy in sends:
        copy.wait_send()
    for here, copy in sends_unless:
        pl.when(jnp.logical_not(here))(copy.wait_send)


def rotate(residual_rows, basis):
    dma = pltpu.SemaphoreType.DMA
    return pl.pallas_call(
        kernel,
        out_shape=[
            jax.ShapeDtypeStruct((16, 4, 4, 64, 128), BF16),
            jax.ShapeDtypeStruct((4, 16, 64, 128), BF16),
        ],
        in_specs=[pl.BlockSpec(memory_space=pltpu.VMEM), pl.BlockSpec(memory_space=pl.ANY)],
        out_specs=[pl.BlockSpec(memory_space=pltpu.VMEM)] * 2,
        scratch_shapes=[
            pltpu.VMEM((BLOCKS, 64, 1024), BF16),
            pltpu.VMEM((1024, 2048), BF16),
            pltpu.VMEM((BLOCKS, 4, 4, 64, 128), F32),
            pltpu.VMEM((BLOCKS, 4, 64, 128), F32),
            pltpu.VMEM((BLOCKS, 2, 4, 64, 128), BF16),
            pltpu.VMEM((BLOCKS, 2, 4, 64, 128), BF16),
            pltpu.VMEM((BLOCKS, 4, 64, 128), BF16),
            pltpu.VMEM((BLOCKS, 4, 64, 128), BF16),
            pltpu.VMEM((BLOCKS, 3, 64, 128), BF16),
            pltpu.VMEM((BLOCKS, 3, 64, 128), BF16),
            pltpu.VMEM((BLOCKS, 64, 128), BF16),
            dma((10,)),
            dma((12,)),
            dma((16,)),
            dma((BLOCKS * 6,)),
            dma((BLOCKS * 6,)),
            dma((BLOCKS * 6,)),
            dma((BLOCKS * 6,)),
            dma((BLOCKS * 4,)),
            dma((BLOCKS * 4,)),
            dma((BLOCKS * 9,)),
            dma((BLOCKS * 9,)),
        ],
        compiler_params=pltpu.CompilerParams(collective_id=0, has_side_effects=True, vmem_limit_bytes=28 * 2**20),
        cost_estimate=pl.CostEstimate(flops=2**31, bytes_accessed=8 * 2**20, transcendentals=0),
    )(residual_rows, basis)


def tile_kernel(columns, panel, tile, right, rows, sem):
    for n in range(4):
        right[:, n * 128 : (n + 1) * 128] = panel[n].reshape(1024, 128)
    copies = []
    for n in range(8):
        left = [columns[:, n // 2, n % 2 * 2 + q].reshape(1024, 128) for q in range(2)]
        out = lax.dot_general(
            jnp.concatenate(left, axis=1), right[...], (((0,), (0,)), ((), ())), preferred_element_type=F32
        )
        part = pl.ds(n * 256, 256)
        rows[part] = out * (1.0 / 1024)
        copies.append(pltpu.make_async_copy(rows.at[part], tile.at[part], sem.at[n]))
        copies[n].start()
    for copy in copies:
        copy.wait()


def body(residual_rows, basis):
    columns, panel = rotate(residual_rows, basis)
    return pl.pallas_call(
        tile_kernel,
        out_shape=jax.ShapeDtypeStruct((2048, 512), F32),
        in_specs=[pl.BlockSpec(memory_space=pltpu.VMEM)] * 2,
        out_specs=pl.BlockSpec(memory_space=pl.ANY),
        scratch_shapes=[
            pltpu.VMEM((1024, 512), BF16),
            pltpu.VMEM((2048, 512), F32),
            pltpu.SemaphoreType.DMA((8,)),
        ],
        compiler_params=pltpu.CompilerParams(vmem_limit_bytes=28 * 2**20),
        cost_estimate=pl.CostEstimate(flops=2**31, bytes_accessed=4 * 2**20, transcendentals=0),
    )(columns, panel)


def solution(mesh):
    return jax.shard_map(
        body,
        mesh=mesh,
        in_specs=(P("col", "tok"), P("tok", "col")),
        out_specs=P("col", "tok"),
        check_vma=False,
    )
```
